32 devices in a mesh: groups: 2 (over x), rows: 16 (over z, y, core).
Axes of the slice: x: 2, y: 2, z: 4, core: 2. Of those that a mesh axis runs over, the one named last changes fastest.
Arguments:
- pair: bfloat16 [512, 256, 128], P(('groups', 'rows')), parts along dimension 0, may hold values from -6 to 6
- proj_weights: bfloat16 [6, 128, 128], replicated, may hold values from -0.5 to 0.5
- cotangent: bfloat16 [512, 256, 128], P(('groups', 'rows')), parts along dimension 0, may hold values from -8.5 to 8.5
Outputs:
- update: bfloat16 [512, 256, 128], P(('groups', 'rows')), parts along dimension 0
- pair_grad: bfloat16 [512, 256, 128], P(('groups', 'rows')), parts along dimension 0
- weight_grads: float32 [12, 128, 128], P('groups'), parts along dimension 0
The draws below stay inside these ranges and needn't reach their ends.
There are 2 independent parts, one for each index of `groups`. The reference program is written for one: setup_inputs(seed, part) draws one part's arguments, and reference() takes and returns one part's arrays. A program takes and returns all parts, laid end to end along the dimension named above; an argument that names none is the same for every part. Nothing has to cross between parts.
All inputs are finite; a program needn't handle non-finite values.
Results may differ from the reference program's by a relative error of at most 0.015.
Values may be sent and summed in bfloat16 or wider, within the bound.
A program may use at most 128 MiB of HBM per device.

```python
import jax
import jax.numpy as jnp
from jax import lax

C = 128
N_RES = 256


def draw_cotangent(key, part):
    first_key = jax.random.fold_in(jax.random.fold_in(key, 7), 0)
    position = jnp.arange(N_RES, dtype=jnp.float32) / (N_RES - 1)
    base_draw = jnp.clip(jax.random.normal(first_key, (N_RES, N_RES, C), jnp.float32), -3.0, 3.0)
    scales = jnp.power(3.0, position)
    values = 0.5 * base_draw * scales[:, None, None]
    return values.astype(jnp.bfloat16)


def levels(rng, shape, cuts, smallest, high):
    factor_of, own = 1.0, jax.random.fold_in(rng, 6)
    for dim, shards_of in cuts:
        heights = jnp.exp(jax.random.uniform(jax.random.fold_in(own, dim), (shards_of,), jnp.float32, smallest / len(cuts), high / len(cuts)))
        factor_of = factor_of * jnp.repeat(heights, shape[dim] // shards_of).reshape([-1 if axis == dim else 1 for axis in range(len(shape))])
    return factor_of


def scatter_about(own_key, extent, width, reach, shards=(), held_as=jnp.bfloat16):
    level = levels(own_key, extent, shards, -0.22, 0.18) if shards else 1.0
    entries = jax.random.normal(own_key, extent, jnp.float32) * width * level
    return jnp.minimum(jnp.maximum(entries, -reach), reach).astype(held_as)


def setup_inputs(seed: int = 0, part: int = 0) -> dict:
    key_of = jax.random.split(jax.random.key(seed), 4)
    own_keys = jax.random.split(jax.random.fold_in(key_of[3], part), 4)
    return {
        "pair": scatter_about(own_keys[0], (N_RES, N_RES, C), 1.0, 6.0, ((0, 16),)),
        "proj_weights": scatter_about(key_of[1], (6, C, C), C ** -0.5, 0.5),
        "cotangent": draw_cotangent(jax.random.fold_in(jax.random.fold_in(key_of[3], part), 71), part),
    }


def layer_norm(values, along_dim):
    centred = values - lax.optimization_barrier(jnp.mean(values, axis=along_dim, keepdims=True))
    inv_scale = lax.rsqrt(lax.optimization_barrier(jnp.mean(centred * centred, axis=along_dim, keepdims=True)) + 1e-05)
    return (centred * inv_scale, inv_scale)

def norm_backward(normed, inv_scale, upstream, along_dim):
    return (upstream - lax.optimization_barrier(jnp.mean(upstream, axis=along_dim, keepdims=True)) - normed * lax.optimization_barrier(jnp.mean(upstream * normed, axis=along_dim, keepdims=True))) * inv_scale

def reference(pair, proj_weights, cotangent):
    residues = pair.shape[0]
    chans = pair.shape[2]
    highest = lax.Precision.HIGHEST
    normed_in, scale_in = layer_norm(pair.astype(jnp.float32), 2)
    normed_bf = normed_in.astype(jnp.bfloat16)
    flat_in = normed_bf.reshape(-1, chans)
    pre_acts = [jnp.dot(flat_in, proj_weights[n], preferred_element_type=jnp.float32) for n in range(5)]
    left_sig = jax.nn.sigmoid(pre_acts[1])
    right_sig = jax.nn.sigmoid(pre_acts[3])
    left_edge = (left_sig * pre_acts[0]).astype(jnp.bfloat16).reshape(residues, residues, chans)
    right_edge = (right_sig * pre_acts[2]).astype(jnp.bfloat16).reshape(residues, residues, chans)
    gating = jax.nn.sigmoid(pre_acts[4])
    left_full = left_edge.astype(jnp.float32)
    right_full = right_edge.astype(jnp.float32)
    products = jnp.einsum('ikc,jkc->ijc', left_full, right_full, precision=highest).astype(jnp.bfloat16)
    normed_mid, scale_mid = layer_norm(products.astype(jnp.float32), 2)
    mid_bf = normed_mid.astype(jnp.bfloat16)
    flat_mid = mid_bf.reshape(-1, chans)
    projected = jnp.dot(flat_mid, proj_weights[5], preferred_element_type=jnp.float32)
    update = (gating * projected).astype(jnp.bfloat16).reshape(residues, residues, chans)
    upstream = cotangent.reshape(-1, chans).astype(jnp.float32)
    gated_up = (upstream * gating).astype(jnp.bfloat16)
    gate_grad = (upstream * projected * gating * (1.0 - gating)).astype(jnp.bfloat16)
    mid_grad = jnp.dot(gated_up, proj_weights[5].T, preferred_element_type=jnp.float32)
    mid_grad = mid_grad.reshape(residues, residues, chans)
    prod_grad = norm_backward(normed_mid, scale_mid, mid_grad, 2).astype(jnp.bfloat16)
    prod_full = prod_grad.astype(jnp.float32)
    left_grad = jnp.einsum('ijc,jkc->ikc', prod_full, right_full, precision=highest).astype(jnp.bfloat16)
    right_grad = jnp.einsum('ijc,ikc->jkc', prod_full, left_full, precision=highest).astype(jnp.bfloat16)
    left_flat = left_grad.reshape(-1, chans).astype(jnp.float32)
    right_flat = right_grad.reshape(-1, chans).astype(jnp.float32)
    edge_grads = [(left_flat * left_sig).astype(jnp.bfloat16), (left_flat * pre_acts[0] * left_sig * (1.0 - left_sig)).astype(jnp.bfloat16), (right_flat * right_sig).astype(jnp.bfloat16), (right_flat * pre_acts[2] * right_sig * (1.0 - right_sig)).astype(jnp.bfloat16), gate_grad]
    input_grad = jnp.zeros((residues * residues, chans), jnp.float32)
    for n in range(5):
        input_grad = input_grad + jnp.dot(edge_grads[n], proj_weights[n].T, preferred_element_type=jnp.float32)
    input_grad = input_grad.reshape(residues, residues, chans)
    pair_grad = norm_backward(normed_in, scale_in, input_grad, 2).astype(jnp.bfloat16)
    grads_list = [jnp.dot(flat_in.T, edge_grads[n], preferred_element_type=jnp.float32) for n in range(5)]
    grads_list.append(jnp.dot(flat_mid.T, gated_up, preferred_element_type=jnp.float32))
    weight_grads = jnp.stack(grads_list) / residues
    return (update, pair_grad, weight_grads)
```

```python
import functools

import jax
import jax.numpy as jnp
from jax import lax
from jax.experimental import pallas as pl
from jax.experimental.pallas import tpu as pltpu
from jax.sharding import PartitionSpec as P

VMEM_LIMIT = 48 * 1024 * 1024
CHUNKS = 4


def layer_norm(values, along_dim):
    centred = values - jnp.mean(values, axis=along_dim, keepdims=True)
    inv_scale = lax.rsqrt(jnp.mean(centred * centred, axis=along_dim, keepdims=True) + 1e-05)
    return (centred * inv_scale, inv_scale)


def norm_backward(normed, inv_scale, upstream, along_dim):
    return (
        upstream
        - jnp.mean(upstream, axis=along_dim, keepdims=True)
        - normed * jnp.mean(upstream * normed, axis=along_dim, keepdims=True)
    ) * inv_scale


def meet(n, me):
    barrier = pltpu.get_barrier_semaphore()

    @pl.loop(1, n)
    def _(s):
        pl.semaphore_signal(
            barrier,
            inc=1,
            device_id={"rows": lax.rem(me + s, n)},
            device_id_type=pl.DeviceIdType.MESH,
        )

    pl.semaphore_wait(barrier, n - 1)


def send(src, dst, send_sem, recv_sem, rank):
    pltpu.make_async_remote_copy(
        src_ref=src,
        dst_ref=dst,
        send_sem=send_sem,
        recv_sem=recv_sem,
        device_id={"rows": rank},
        device_id_type=pl.DeviceIdType.MESH,
    ).start()


def drain(ref, sem):
    pltpu.make_async_copy(ref, ref, sem).wait()


def forward_kernel(
    n, left, right, regrouped, left_held, right_held, products, send_sem, recv_sem, back_send, back_recv
):
    me = lax.axis_index("rows")
    width, rows = left.shape[1], left.shape[2]
    chunks = recv_sem.shape[1]
    per = width // chunks
    meet(n, me)
    mine = pl.ds(me * rows, rows)
    for g in range(chunks):
        part = pl.ds(g * per, per)
        for a, (src, dst) in enumerate(((left, left_held), (right, right_held))):
            pltpu.make_async_copy(
                src.at[me, part], dst.at[part, mine, :], recv_sem.at[a, g]
            ).start()

        @pl.loop(1, n)
        def _(s):
            rank = lax.rem(me + s, n)
            for a, (src, dst) in enumerate(((left, left_held), (right, right_held))):
                send(
                    src.at[rank, part],
                    dst.at[part, mine, :],
                    send_sem.at[a],
                    recv_sem.at[a, g],
                    rank,
                )

    for g in range(chunks):
        part = pl.ds(g * per, per)
        drain(left_held.at[part], recv_sem.at[0, g])
        drain(right_held.at[part], recv_sem.at[1, g])

        @pl.loop(g * per, (g + 1) * per)
        def _(c):
            products[c] = lax.dot_general(
                left_held[c], right_held[c], (((1,), (1,)), ((), ())),
                preferred_element_type=jnp.float32,
            ).astype(jnp.bfloat16)

        pltpu.make_async_copy(
            products.at[part, mine, :], regrouped.at[me, part], back_recv
        ).start()

        @pl.loop(1, n)
        def _(s):
            rank = lax.rem(me + s, n)
            send(
                products.at[part, pl.ds(rank * rows, rows), :],
                regrouped.at[me, part],
                back_send,
                back_recv,
                rank,
            )

    drain(regrouped, back_recv)
    others = pl.ds(0, n - 1)
    drain(left.at[others], send_sem.at[0])
    drain(right.at[others], send_sem.at[1])
    drain(left.at[others], back_send)


def backward_kernel(
    n, grad, left_held, right_held, left_back, right_back,
    held, left_part, right_part, send_sem, recv_sem, back_send, back_recv
):
    me = lax.axis_index("rows")
    width, rows = grad.shape[1], grad.shape[2]
    chunks = recv_sem.shape[0]
    per = width // chunks
    meet(n, me)
    mine = pl.ds(me * rows, rows)
    for g in range(chunks):
        part = pl.ds(g * per, per)
        pltpu.make_async_copy(grad.at[me, part], held.at[part, mine, :], recv_sem.at[g]).start()

        @pl.loop(1, n)
        def _(s):
            rank = lax.rem(me + s, n)
            send(grad.at[rank, part], held.at[part, mine, :], send_sem, recv_sem.at[g], rank)

    for g in range(chunks):
        part = pl.ds(g * per, per)
        drain(held.at[part], recv_sem.at[g])

        @pl.loop(g * per, (g + 1) * per)
        def _(c):
            left_part[c] = lax.dot_general(
                held[c], right_held[c], (((1,), (0,)), ((), ())),
                preferred_element_type=jnp.float32,
            ).astype(jnp.bfloat16)
            right_part[c] = lax.dot_general(
                held[c], left_held[c], (((0,), (0,)), ((), ())),
                preferred_element_type=jnp.float32,
            ).astype(jnp.bfloat16)

        both = ((left_part, left_back), (right_part, right_back))
        for a, (src, dst) in enumerate(both):
            pltpu.make_async_copy(
                src.at[part, mine, :], dst.at[me, part], back_recv.at[a]
            ).start()

        @pl.loop(1, n)
        def _(s):
            rank = lax.rem(me + s, n)
            for a, (src, dst) in enumerate(both):
                send(
                    src.at[part, pl.ds(rank * rows, rows), :],
                    dst.at[me, part],
                    back_send.at[a],
                    back_recv.at[a],
                    rank,
                )

    drain(left_back, back_recv.at[0])
    drain(right_back, back_recv.at[1])
    others = pl.ds(0, n - 1)
    drain(grad.at[others], send_sem)
    drain(grad.at[others], back_send.at[0])
    drain(grad.at[others], back_send.at[1])


def totals_kernel(n, shares, totals, landed, mine, send_sem, recv_sem, back_send, back_recv):
    me = lax.axis_index("rows")
    meet(n, me)
    pltpu.make_async_copy(shares.at[me], landed.at[me], recv_sem).start()

    @pl.loop(1, n)
    def _(s):
        rank = lax.rem(me + s, n)
        send(shares.at[rank], landed.at[me], send_sem, recv_sem, rank)

    drain(landed, recv_sem)
    mine[...] = jnp.sum(landed[...].astype(jnp.float32), axis=0).astype(mine.dtype)
    pltpu.make_async_copy(mine, totals.at[me], back_recv).start()

    @pl.loop(1, n)
    def _(s):
        rank = lax.rem(me + s, n)
        send(mine, totals.at[me], back_send, back_recv, rank)

    drain(totals, back_recv)
    others = pl.ds(0, n - 1)
    drain(shares.at[others], send_sem)
    drain(shares.at[others], back_send)


def in_vmem(count):
    return [pl.BlockSpec(memory_space=pltpu.VMEM)] * count


def params(collective_id):
    return pltpu.CompilerParams(
        collective_id=collective_id, has_side_effects=True, vmem_limit_bytes=VMEM_LIMIT
    )


def exchange_forward(left, right):
    n, width, rows, residues = left.shape
    chunks = min(CHUNKS, width)
    slab = jax.ShapeDtypeStruct((width, n * rows, residues), jnp.bfloat16)
    whole = jax.ShapeDtypeStruct((width, n * rows, n * rows), jnp.bfloat16)
    return pl.pallas_call(
        functools.partial(forward_kernel, n),
        out_shape=[jax.ShapeDtypeStruct((n, width, rows, n * rows), jnp.bfloat16), slab, slab],
        in_specs=in_vmem(2),
        out_specs=in_vmem(3),
        scratch_shapes=[
            pltpu.VMEM(whole.shape, jnp.bfloat16),
            pltpu.SemaphoreType.DMA((2,)),
            pltpu.SemaphoreType.DMA((2, chunks)),
            pltpu.SemaphoreType.DMA,
            pltpu.SemaphoreType.DMA,
        ],
        compiler_params=params(0),
    )(left, right)


def exchange_backward(grad, left_held, right_held):
    n, width, rows, residues = grad.shape
    chunks = min(CHUNKS, width)
    slab = (width, n * rows, residues)
    back = jax.ShapeDtypeStruct((n, width, rows, residues), jnp.bfloat16)
    return pl.pallas_call(
        functools.partial(backward_kernel, n),
        out_shape=[back, back],
        in_specs=in_vmem(3),
        out_specs=in_vmem(2),
        scratch_shapes=[pltpu.VMEM(slab, jnp.bfloat16)] * 3
        + [
            pltpu.SemaphoreType.DMA,
            pltpu.SemaphoreType.DMA((chunks,)),
            pltpu.SemaphoreType.DMA((2,)),
            pltpu.SemaphoreType.DMA((2,)),
        ],
        compiler_params=params(1),
    )(grad, left_held, right_held)


def sum_over_rows(shares, n):
    count, chans, _ = shares.shape
    rows = count * chans // n
    dtype = jnp.bfloat16 if rows % 16 == 0 else jnp.float32
    shares = shares.astype(jnp.bfloat16).astype(dtype).reshape(n, rows, chans)
    totals = pl.pallas_call(
        functools.partial(totals_kernel, n),
        out_shape=jax.ShapeDtypeStruct(shares.shape, dtype),
        in_specs=in_vmem(1),
        out_specs=pl.BlockSpec(memory_space=pltpu.VMEM),
        scratch_shapes=[
            pltpu.VMEM(shares.shape, dtype),
            pltpu.VMEM((rows, chans), dtype),
            pltpu.SemaphoreType.DMA,
            pltpu.SemaphoreType.DMA,
            pltpu.SemaphoreType.DMA,
            pltpu.SemaphoreType.DMA,
        ],
        compiler_params=params(2),
    )(shares)
    return totals.reshape(count, chans, chans).astype(jnp.float32)


def body(pair, proj_weights, cotangent):
    residues = pair.shape[1]
    local_rows = pair.shape[0]
    chans = pair.shape[2]
    ranks = lax.axis_size("rows")
    slab_width = chans // ranks
    normed_in, scale_in = layer_norm(pair.astype(jnp.float32), 2)
    normed_bf = normed_in.astype(jnp.bfloat16)
    edge_pre = jnp.einsum(
        "ikd,ndc->ncik", normed_bf, proj_weights[0:4], preferred_element_type=jnp.float32
    )
    gate_pre = jnp.einsum(
        "ikd,dc->ikc", normed_bf, proj_weights[4], preferred_element_type=jnp.float32
    )
    left_sig = jax.nn.sigmoid(edge_pre[1])
    right_sig = jax.nn.sigmoid(edge_pre[3])
    left_edge = (
        (left_sig * edge_pre[0])
        .astype(jnp.bfloat16)
        .reshape(ranks, slab_width, local_rows, residues)
    )
    right_edge = (
        (right_sig * edge_pre[2])
        .astype(jnp.bfloat16)
        .reshape(ranks, slab_width, local_rows, residues)
    )
    regrouped, left_held, right_held = exchange_forward(left_edge, right_edge)
    regrouped = regrouped.reshape(chans, local_rows, residues)
    normed_mid, scale_mid = layer_norm(regrouped.astype(jnp.float32), 0)
    mid_bf = normed_mid.astype(jnp.bfloat16)
    projected = jnp.einsum(
        "cij,cd->ijd", mid_bf, proj_weights[5], preferred_element_type=jnp.float32
    )
    gating = jax.nn.sigmoid(gate_pre)
    update = (gating * projected).astype(jnp.bfloat16)
    upstream = cotangent.astype(jnp.float32)
    gated_up = (upstream * gating).astype(jnp.bfloat16)
    gate_grad = (upstream * projected * gating * (1.0 - gating)).astype(jnp.bfloat16)
    out_weights = jnp.stack(
        [
            jnp.einsum("ikd,ikc->dc", normed_bf, gate_grad, preferred_element_type=jnp.float32),
            jnp.einsum("cij,ijd->cd", mid_bf, gated_up, preferred_element_type=jnp.float32),
        ]
    )
    mid_grad = jnp.einsum(
        "ijd,cd->cij", gated_up, proj_weights[5], preferred_element_type=jnp.float32
    )
    prod_grad = norm_backward(normed_mid, scale_mid, mid_grad, 0).astype(jnp.bfloat16)
    prod_grad = prod_grad.reshape(ranks, slab_width, local_rows, residues)
    left_back, right_back = exchange_backward(prod_grad, left_held, right_held)
    left_full = left_back.reshape(chans, local_rows, residues).astype(jnp.float32)
    right_full = right_back.reshape(chans, local_rows, residues).astype(jnp.float32)
    edge_grad = jnp.stack(
        [
            left_full * left_sig,
            left_full * edge_pre[0] * left_sig * (1.0 - left_sig),
            right_full * right_sig,
            right_full * edge_pre[2] * right_sig * (1.0 - right_sig),
        ]
    ).astype(jnp.bfloat16)
    in_weights = jnp.einsum(
        "ikd,ncik->ndc", normed_bf, edge_grad, preferred_element_type=jnp.float32
    )
    input_grad = jnp.einsum(
        "ncik,ndc->ikd", edge_grad, proj_weights[0:4], preferred_element_type=jnp.float32
    )
    input_grad = input_grad + jnp.einsum(
        "ikc,dc->ikd", gate_grad, proj_weights[4], preferred_element_type=jnp.float32
    )
    pair_grad = norm_backward(normed_in, scale_in, input_grad, 2).astype(jnp.bfloat16)
    totals = sum_over_rows(jnp.concatenate([in_weights, out_weights], axis=0), ranks)
    weight_grads = totals / residues
    return (update, pair_grad, weight_grads)


def solution(mesh):
    in_specs = (P(("groups", "rows"), None, None), P(), P(("groups", "rows"), None, None))
    out_specs = (
        P(("groups", "rows"), None, None),
        P(("groups", "rows"), None, None),
        P("groups", None, None),
    )
    return jax.shard_map(body, mesh=mesh, in_specs=in_specs, out_specs=out_specs, check_vma=False)
```

```python
import functools

import jax
import jax.numpy as jnp
from jax import lax
from jax.experimental import pallas as pl
from jax.experimental.pallas import tpu as pltpu
from jax.sharding import PartitionSpec as P

VMEM_LIMIT = 48 * 1024 * 1024
CHUNKS = 8


def layer_norm(values, along_dim):
    centred = values - jnp.mean(values, axis=along_dim, keepdims=True)
    inv_scale = lax.rsqrt(jnp.mean(centred * centred, axis=along_dim, keepdims=True) + 1e-05)
    return (centred * inv_scale, inv_scale)


def norm_backward(normed, inv_scale, upstream, along_dim):
    return (
        upstream
        - jnp.mean(upstream, axis=along_dim, keepdims=True)
        - normed * jnp.mean(upstream * normed, axis=along_dim, keepdims=True)
    ) * inv_scale


def meet(n, me):
    barrier = pltpu.get_barrier_semaphore()

    @pl.loop(1, n)
    def _(s):
        pl.semaphore_signal(
            barrier,
            inc=1,
            device_id={"rows": lax.rem(me + s, n)},
            device_id_type=pl.DeviceIdType.MESH,
        )

    pl.semaphore_wait(barrier, n - 1)


def send(src, dst, send_sem, recv_sem, rank):
    pltpu.make_async_remote_copy(
        src_ref=src,
        dst_ref=dst,
        send_sem=send_sem,
        recv_sem=recv_sem,
        device_id={"rows": rank},
        device_id_type=pl.DeviceIdType.MESH,
    ).start()


def drain(ref, sem):
    pltpu.make_async_copy(ref, ref, sem).wait()


def place(n):
    me = lax.axis_index("rows")
    half = lax.div(me, n // 2)
    first = half * (n // 2)
    hub = n // 4 * (1 + half)
    is_hub = jnp.logical_and(me >= hub, me < hub + n // 4)
    partner = me + n // 4 * (1 - 2 * half)
    return me, half, first, hub, is_hub, partner


def to_hubs(me, hub, hubs, is_hub, pairs, part, send_sems, recv_sems):
    @pl.loop(0, hubs)
    def _(s):
        q = lax.rem(me + s, hubs)

        @pl.when(hub + q != me)
        def _():
            for (src, dst), sent, came in zip(pairs, send_sems, recv_sems):
                send(src.at[q, part], dst, sent, came, hub + q)

    @pl.when(is_hub)
    def _():
        for (src, dst), came in zip(pairs, recv_sems):
            pltpu.make_async_copy(src.at[me - hub, part], dst, came).start()


def from_hub(me, first, hub, members, rows, pairs, part, send_sems, recv_sems):
    for (src, dst), came in zip(pairs, recv_sems):
        pltpu.make_async_copy(
            src.at[part, pl.ds((me - first) * rows, rows), :], dst.at[me - hub, part], came
        ).start()

    @pl.loop(1, members)
    def _(s):
        member = lax.rem(me - first + s, members)
        for (src, dst), sent, came in zip(pairs, send_sems, recv_sems):
            send(
                src.at[part, pl.ds(member * rows, rows), :],
                dst.at[me - hub, part],
                sent,
                came,
                first + member,
            )


def forward_kernel(
    n, left, right, regrouped, left_held, right_held, products,
    send_sem, recv_sem, swap_send, swap_recv, back_send, back_recv
):
    me, half, first, hub, is_hub, partner = place(n)
    hubs, width, rows, _ = left.shape
    members = n // 2
    chunks = swap_recv.shape[0]
    per = width // chunks
    meet(n, me)
    own_rows = pl.ds(first * rows, members * rows)
    far_rows = pl.ds((members - first) * rows, members * rows)
    for g in range(chunks):
        part = pl.ds(g * per, per)
        pairs = (
            (right, right_held.at[part, pl.ds(me * rows, rows), :]),
            (left, left_held.at[part, pl.ds((me - first) * rows, rows), :]),
        )
        to_hubs(
            me, hub, hubs, is_hub, pairs, part,
            (send_sem.at[1], send_sem.at[0]), (recv_sem.at[1, g], recv_sem.at[0, g]),
        )

    @pl.when(is_hub)
    def _():
        for g in range(chunks + 1):
            if g < chunks:
                part = pl.ds(g * per, per)
                block = right_held.at[part, own_rows, :]
                drain(block, recv_sem.at[1, g])
                send(block, block, swap_send, swap_recv.at[g], partner)
            if g > 0:
                done = pl.ds((g - 1) * per, per)
                drain(left_held.at[done], recv_sem.at[0, g - 1])
                drain(right_held.at[done, far_rows, :], swap_recv.at[g - 1])

                @pl.loop((g - 1) * per, g * per)
                def _(c):
                    products[c] = lax.dot_general(
                        left_held[c], right_held[c], (((1,), (1,)), ((), ())),
                        preferred_element_type=jnp.float32,
                    ).astype(jnp.bfloat16)

                from_hub(
                    me, first, hub, members, rows, ((products, regrouped),), done,
                    (back_send,), (back_recv,),
                )

    drain(regrouped, back_recv)

    @pl.when(is_hub)
    def _():
        others = pl.ds(0, hubs - 1)
        drain(left.at[others], send_sem.at[0])
        drain(right.at[others], send_sem.at[1])
        drain(left_held, swap_send)
        drain(products.at[:, pl.ds(0, (members - 1) * rows), :], back_send)

    @pl.when(jnp.logical_not(is_hub))
    def _():
        drain(left, send_sem.at[0])
        drain(right, send_sem.at[1])


def backward_kernel(
    n, grad, left_held, right_held, left_back, right_back,
    held, left_part, kept, away, landed,
    send_sem, recv_sem, swap_send, swap_recv, back_send, back_recv
):
    me, half, first, hub, is_hub, partner = place(n)
    hubs, width, rows, _ = grad.shape
    members = n // 2
    chunks = swap_recv.shape[0]
    per = width // chunks
    meet(n, me)
    span = members * rows
    own_cols = pl.ds(pl.multiple_of(first * rows, span), span)
    far_cols = pl.ds(pl.multiple_of((members - first) * rows, span), span)
    for g in range(chunks):
        part = pl.ds(g * per, per)
        pairs = ((grad, held.at[part, pl.ds((me - first) * rows, rows), :]),)
        to_hubs(me, hub, hubs, is_hub, pairs, part, (send_sem,), (recv_sem.at[g],))

    def outer(upstream, values):
        return lax.dot_general(
            upstream, values, (((0,), (0,)), ((), ())), preferred_element_type=jnp.float32
        ).astype(jnp.bfloat16)

    @pl.when(is_hub)
    def _():
        for g in range(chunks + 1):
            if g < chunks:
                part = pl.ds(g * per, per)
                drain(held.at[part], recv_sem.at[g])

                @pl.loop(g * per, (g + 1) * per)
                def _(c):
                    away[c] = outer(held[c, :, far_cols], left_held[c])

                send(away.at[part], landed.at[part], swap_send, swap_recv.at[g], partner)

                @pl.loop(g * per, (g + 1) * per)
                def _(c):
                    left_part[c] = lax.dot_general(
                        held[c], right_held[c], (((1,), (0,)), ((), ())),
                        preferred_element_type=jnp.float32,
                    ).astype(jnp.bfloat16)
                    kept[c] = outer(held[c, :, own_cols], left_held[c])

                from_hub(
                    me, first, hub, members, rows, ((left_part, left_back),), part,
                    (back_send.at[0],), (back_recv.at[0],),
                )
            if g > 0:
                done = pl.ds((g - 1) * per, per)
                drain(landed.at[done], swap_recv.at[g - 1])

                @pl.loop((g - 1) * per, g * per)
                def _(c):
                    kept[c] = (
                        kept[c].astype(jnp.float32) + landed[c].astype(jnp.float32)
                    ).astype(jnp.bfloat16)

                from_hub(
                    me, first, hub, members, rows, ((kept, right_back),), done,
                    (back_send.at[1],), (back_recv.at[1],),
                )

    drain(left_back, back_recv.at[0])
    drain(right_back, back_recv.at[1])

    @pl.when(is_hub)
    def _():
        drain(grad.at[pl.ds(0, hubs - 1)], send_sem)
        drain(away, swap_send)
        others = pl.ds(0, (members - 1) * rows)
        drain(left_part.at[:, others, :], back_send.at[0])
        drain(kept.at[:, others, :], back_send.at[1])

    @pl.when(jnp.logical_not(is_hub))
    def _():
        drain(grad, send_sem)


def totals_kernel(n, shares, totals, landed, mine, send_sem, recv_sem, back_send, back_recv):
    me = lax.axis_index("rows")
    meet(n, me)
    pltpu.make_async_copy(shares.at[me], landed.at[me], recv_sem).start()

    @pl.loop(1, n)
    def _(s):
        rank = lax.rem(me + s, n)
        send(shares.at[rank], landed.at[me], send_sem, recv_sem, rank)

    drain(landed, recv_sem)
    mine[...] = jnp.sum(landed[...].astype(jnp.float32), axis=0).astype(mine.dtype)
    pltpu.make_async_copy(mine, totals.at[me], back_recv).start()

    @pl.loop(1, n)
    def _(s):
        rank = lax.rem(me + s, n)
        send(mine, totals.at[me], back_send, back_recv, rank)

    drain(totals, back_recv)
    others = pl.ds(0, n - 1)
    drain(shares.at[others], send_sem)
    drain(shares.at[others], back_send)


def in_vmem(count):
    return [pl.BlockSpec(memory_space=pltpu.VMEM)] * count


def params(collective_id):
    return pltpu.CompilerParams(
        collective_id=collective_id, has_side_effects=True, vmem_limit_bytes=VMEM_LIMIT
    )


def exchange_forward(left, right, n):
    hubs, width, rows, residues = left.shape
    chunks = min(CHUNKS, width)
    return pl.pallas_call(
        functools.partial(forward_kernel, n),
        out_shape=[
            jax.ShapeDtypeStruct((hubs, width, rows, n * rows), jnp.bfloat16),
            jax.ShapeDtypeStruct((width, n // 2 * rows, residues), jnp.bfloat16),
            jax.ShapeDtypeStruct((width, n * rows, residues), jnp.bfloat16),
        ],
        in_specs=in_vmem(2),
        out_specs=in_vmem(3),
        scratch_shapes=[
            pltpu.VMEM((width, n // 2 * rows, n * rows), jnp.bfloat16),
            pltpu.SemaphoreType.DMA((2,)),
            pltpu.SemaphoreType.DMA((2, chunks)),
            pltpu.SemaphoreType.DMA,
            pltpu.SemaphoreType.DMA((chunks,)),
            pltpu.SemaphoreType.DMA,
            pltpu.SemaphoreType.DMA,
        ],
        compiler_params=params(0),
    )(left, right)


def exchange_backward(grad, left_held, right_held, n):
    hubs, width, rows, _ = grad.shape
    residues = left_held.shape[2]
    chunks = min(CHUNKS, width)
    slab = (width, n // 2 * rows, residues)
    back = jax.ShapeDtypeStruct((hubs, width, rows, residues), jnp.bfloat16)
    return pl.pallas_call(
        functools.partial(backward_kernel, n),
        out_shape=[back, back],
        in_specs=in_vmem(3),
        out_specs=in_vmem(2),
        scratch_shapes=[pltpu.VMEM((width, n // 2 * rows, n * rows), jnp.bfloat16)]
        + [pltpu.VMEM(slab, jnp.bfloat16)] * 4
        + [
            pltpu.SemaphoreType.DMA,
            pltpu.SemaphoreType.DMA((chunks,)),
            pltpu.SemaphoreType.DMA,
            pltpu.SemaphoreType.DMA((chunks,)),
            pltpu.SemaphoreType.DMA((2,)),
            pltpu.SemaphoreType.DMA((2,)),
        ],
        compiler_params=params(1),
    )(grad, left_held, right_held)


def sum_over_rows(shares, n):
    count, chans, _ = shares.shape
    rows = count * chans // n
    dtype = jnp.bfloat16 if rows % 16 == 0 else jnp.float32
    shares = shares.astype(jnp.bfloat16).astype(dtype).reshape(n, rows, chans)
    totals = pl.pallas_call(
        functools.partial(totals_kernel, n),
        out_shape=jax.ShapeDtypeStruct(shares.shape, dtype),
        in_specs=in_vmem(1),
        out_specs=pl.BlockSpec(memory_space=pltpu.VMEM),
        scratch_shapes=[
            pltpu.VMEM(shares.shape, dtype),
            pltpu.VMEM((rows, chans), dtype),
            pltpu.SemaphoreType.DMA,
            pltpu.SemaphoreType.DMA,
            pltpu.SemaphoreType.DMA,
            pltpu.SemaphoreType.DMA,
        ],
        compiler_params=params(2),
    )(shares)
    return totals.reshape(count, chans, chans).astype(jnp.float32)


def body(pair, proj_weights, cotangent):
    residues = pair.shape[1]
    local_rows = pair.shape[0]
    chans = pair.shape[2]
    ranks = lax.axis_size("rows")
    hubs = ranks // 4
    slab_width = chans // hubs
    normed_in, scale_in = layer_norm(pair.astype(jnp.float32), 2)
    normed_bf = normed_in.astype(jnp.bfloat16)
    edge_pre = jnp.einsum(
        "ikd,ndc->ncik", normed_bf, proj_weights[0:4], preferred_element_type=jnp.float32
    )
    gate_pre = jnp.einsum(
        "ikd,dc->ikc", normed_bf, proj_weights[4], preferred_element_type=jnp.float32
    )
    left_sig = jax.nn.sigmoid(edge_pre[1])
    right_sig = jax.nn.sigmoid(edge_pre[3])
    left_edge = (
        (left_sig * edge_pre[0])
        .astype(jnp.bfloat16)
        .reshape(hubs, slab_width, local_rows, residues)
    )
    right_edge = (
        (right_sig * edge_pre[2])
        .astype(jnp.bfloat16)
        .reshape(hubs, slab_width, local_rows, residues)
    )
    regrouped, left_held, right_held = exchange_forward(left_edge, right_edge, ranks)
    regrouped = regrouped.reshape(chans, local_rows, residues)
    normed_mid, scale_mid = layer_norm(regrouped.astype(jnp.float32), 0)
    mid_bf = normed_mid.astype(jnp.bfloat16)
    projected = jnp.einsum(
        "cij,cd->ijd", mid_bf, proj_weights[5], preferred_element_type=jnp.float32
    )
    gating = jax.nn.sigmoid(gate_pre)
    update = (gating * projected).astype(jnp.bfloat16)
    upstream = cotangent.astype(jnp.float32)
    gated_up = (upstream * gating).astype(jnp.bfloat16)
    gate_grad = (upstream * projected * gating * (1.0 - gating)).astype(jnp.bfloat16)
    out_weights = jnp.stack(
        [
            jnp.einsum("ikd,ikc->dc", normed_bf, gate_grad, preferred_element_type=jnp.float32),
            jnp.einsum("cij,ijd->cd", mid_bf, gated_up, preferred_element_type=jnp.float32),
        ]
    )
    mid_grad = jnp.einsum(
        "ijd,cd->cij", gated_up, proj_weights[5], preferred_element_type=jnp.float32
    )
    prod_grad = norm_backward(normed_mid, scale_mid, mid_grad, 0).astype(jnp.bfloat16)
    prod_grad = prod_grad.reshape(hubs, slab_width, local_rows, residues)
    left_back, right_back = exchange_backward(prod_grad, left_held, right_held, ranks)
    left_full = left_back.reshape(chans, local_rows, residues).astype(jnp.float32)
    right_full = right_back.reshape(chans, local_rows, residues).astype(jnp.float32)
    edge_grad = jnp.stack(
        [
            left_full * left_sig,
            left_full * edge_pre[0] * left_sig * (1.0 - left_sig),
            right_full * right_sig,
            right_full * edge_pre[2] * right_sig * (1.0 - right_sig),
        ]
    ).astype(jnp.bfloat16)
    in_weights = jnp.einsum(
        "ikd,ncik->ndc", normed_bf, edge_grad, preferred_element_type=jnp.float32
    )
    input_grad = jnp.einsum(
        "ncik,ndc->ikd", edge_grad, proj_weights[0:4], preferred_element_type=jnp.float32
    )
    input_grad = input_grad + jnp.einsum(
        "ikc,dc->ikd", gate_grad, proj_weights[4], preferred_element_type=jnp.float32
    )
    pair_grad = norm_backward(normed_in, scale_in, input_grad, 2).astype(jnp.bfloat16)
    totals = sum_over_rows(jnp.concatenate([in_weights, out_weights], axis=0), ranks)
    weight_grads = totals / residues
    return (update, pair_grad, weight_grads)


def solution(mesh):
    in_specs = (P(("groups", "rows"), None, None), P(), P(("groups", "rows"), None, None))
    out_specs = (
        P(("groups", "rows"), None, None),
        P(("groups", "rows"), None, None),
        P("groups", None, None),
    )
    return jax.shard_map(body, mesh=mesh, in_specs=in_specs, out_specs=out_specs, check_vma=False)
```

```python
import functools

import jax
import jax.numpy as jnp
from jax import lax
from jax.experimental import pallas as pl
from jax.experimental.pallas import tpu as pltpu
from jax.sharding import PartitionSpec as P

VMEM_LIMIT = 48 * 1024 * 1024
CHUNKS = 16


def layer_norm(values, along_dim):
    centred = values - jnp.mean(values, axis=along_dim, keepdims=True)
    inv_scale = lax.rsqrt(jnp.mean(centred * centred, axis=along_dim, keepdims=True) + 1e-05)
    return (centred * inv_scale, inv_scale)


def norm_backward(normed, inv_scale, upstream, along_dim):
    return (
        upstream
        - jnp.mean(upstream, axis=along_dim, keepdims=True)
        - normed * jnp.mean(upstream * normed, axis=along_dim, keepdims=True)
    ) * inv_scale


def meet(n, me):
    barrier = pltpu.get_barrier_semaphore()

    @pl.loop(1, n)
    def _(s):
        pl.semaphore_signal(
            barrier,
            inc=1,
            device_id={"rows": lax.rem(me + s, n)},
            device_id_type=pl.DeviceIdType.MESH,
        )

    pl.semaphore_wait(barrier, n - 1)


def send(src, dst, send_sem, recv_sem, rank):
    pltpu.make_async_remote_copy(
        src_ref=src,
        dst_ref=dst,
        send_sem=send_sem,
        recv_sem=recv_sem,
        device_id={"rows": rank},
        device_id_type=pl.DeviceIdType.MESH,
    ).start()


def drain(ref, sem):
    pltpu.make_async_copy(ref, ref, sem).wait()


def place(n):
    me = lax.axis_index("rows")
    half = lax.div(me, n // 2)
    first = half * (n // 2)
    hub = n // 4 * (1 + half)
    is_hub = jnp.logical_and(me >= hub, me < hub + n // 4)
    partner = me + n // 4 * (1 - 2 * half)
    return me, half, first, hub, is_hub, partner


def to_hubs(me, hub, hubs, is_hub, pairs, part, send_sems, recv_sems):
    @pl.loop(0, hubs)
    def _(s):
        q = lax.rem(me + s, hubs)

        @pl.when(hub + q != me)
        def _():
            for (src, dst), sent, came in zip(pairs, send_sems, recv_sems):
                send(src.at[q, part], dst, sent, came, hub + q)

    @pl.when(is_hub)
    def _():
        for (src, dst), came in zip(pairs, recv_sems):
            pltpu.make_async_copy(src.at[me - hub, part], dst, came).start()


def from_hub(me, first, hub, members, rows, pairs, part, send_sems, recv_sems):
    for (src, dst), came in zip(pairs, recv_sems):
        pltpu.make_async_copy(
            src.at[part, pl.ds((me - first) * rows, rows), :], dst.at[me - hub, part], came
        ).start()

    @pl.loop(1, members)
    def _(s):
        member = lax.rem(me - first + s, members)
        for (src, dst), sent, came in zip(pairs, send_sems, recv_sems):
            send(
                src.at[part, pl.ds(member * rows, rows), :],
                dst.at[me - hub, part],
                sent,
                came,
                first + member,
            )


def forward_kernel(
    n, left, right, regrouped, left_held, right_held, products,
    send_sem, recv_sem, swap_send, swap_recv, back_send, back_recv
):
    me, half, first, hub, is_hub, partner = place(n)
    hubs, width, rows, _ = left.shape
    members = n // 2
    chunks = swap_recv.shape[0]
    per = width // chunks
    meet(n, me)
    own_rows = pl.ds(first * rows, members * rows)
    far_rows = pl.ds((members - first) * rows, members * rows)
    for g in range(chunks):
        part = pl.ds(g * per, per)
        pairs = (
            (right, right_held.at[part, pl.ds(me * rows, rows), :]),
            (left, left_held.at[part, pl.ds((me - first) * rows, rows), :]),
        )
        to_hubs(
            me, hub, hubs, is_hub, pairs, part,
            (send_sem.at[1], send_sem.at[0]), (recv_sem.at[1, g], recv_sem.at[0, g]),
        )

    @pl.when(is_hub)
    def _():
        for g in range(chunks + 1):
            if g < chunks:
                part = pl.ds(g * per, per)
                block = right_held.at[part, own_rows, :]
                drain(block, recv_sem.at[1, g])
                send(block, block, swap_send, swap_recv.at[g], partner)
            if g > 0:
                done = pl.ds((g - 1) * per, per)
                drain(left_held.at[done], recv_sem.at[0, g - 1])
                drain(right_held.at[done, far_rows, :], swap_recv.at[g - 1])

                @pl.loop((g - 1) * per, g * per)
                def _(c):
                    products[c] = lax.dot_general(
                        left_held[c], right_held[c], (((1,), (1,)), ((), ())),
                        preferred_element_type=jnp.float32,
                    ).astype(jnp.bfloat16)

                from_hub(
                    me, first, hub, members, rows, ((products, regrouped),), done,
                    (back_send,), (back_recv,),
                )

    drain(regrouped, back_recv)

    @pl.when(is_hub)
    def _():
        others = pl.ds(0, hubs - 1)
        drain(left.at[others], send_sem.at[0])
        drain(right.at[others], send_sem.at[1])
        drain(left_held, swap_send)
        drain(products.at[:, pl.ds(0, (members - 1) * rows), :], back_send)

    @pl.when(jnp.logical_not(is_hub))
    def _():
        drain(left, send_sem.at[0])
        drain(right, send_sem.at[1])


def backward_kernel(
    n, grad, left_held, right_held, left_back, right_back,
    held, left_part, kept, away, landed,
    send_sem, recv_sem, swap_send, swap_recv, back_send, back_recv
):
    me, half, first, hub, is_hub, partner = place(n)
    hubs, width, rows, _ = grad.shape
    members = n // 2
    chunks = swap_recv.shape[0]
    per = width // chunks
    meet(n, me)
    span = members * rows
    own_cols = pl.ds(pl.multiple_of(first * rows, span), span)
    far_cols = pl.ds(pl.multiple_of((members - first) * rows, span), span)
    for g in range(chunks):
        part = pl.ds(g * per, per)
        pairs = ((grad, held.at[part, pl.ds((me - first) * rows, rows), :]),)
        to_hubs(me, hub, hubs, is_hub, pairs, part, (send_sem,), (recv_sem.at[g],))

    def outer(upstream, values):
        return lax.dot_general(
            upstream, values, (((0,), (0,)), ((), ())), preferred_element_type=jnp.float32
        ).astype(jnp.bfloat16)

    @pl.when(is_hub)
    def _():
        for g in range(chunks + 1):
            if g < chunks:
                part = pl.ds(g * per, per)
                drain(held.at[part], recv_sem.at[g])

                @pl.loop(g * per, (g + 1) * per)
                def _(c):
                    away[c] = outer(held[c, :, far_cols], left_held[c])

                send(away.at[part], landed.at[part], swap_send, swap_recv.at[g], partner)

                @pl.loop(g * per, (g + 1) * per)
                def _(c):
                    left_part[c] = lax.dot_general(
                        held[c], right_held[c], (((1,), (0,)), ((), ())),
                        preferred_element_type=jnp.float32,
                    ).astype(jnp.bfloat16)
                    kept[c] = outer(held[c, :, own_cols], left_held[c])

                from_hub(
                    me, first, hub, members, rows, ((left_part, left_back),), part,
                    (back_send.at[0],), (back_recv.at[0],),
                )
            if g > 0:
                done = pl.ds((g - 1) * per, per)
                drain(landed.at[done], swap_recv.at[g - 1])

                @pl.loop((g - 1) * per, g * per)
                def _(c):
                    kept[c] = (
                        kept[c].astype(jnp.float32) + landed[c].astype(jnp.float32)
                    ).astype(jnp.bfloat16)

                from_hub(
                    me, first, hub, members, rows, ((kept, right_back),), done,
                    (back_send.at[1],), (back_recv.at[1],),
                )

    drain(left_back, back_recv.at[0])
    drain(right_back, back_recv.at[1])

    @pl.when(is_hub)
    def _():
        drain(grad.at[pl.ds(0, hubs - 1)], send_sem)
        drain(away, swap_send)
        others = pl.ds(0, (members - 1) * rows)
        drain(left_part.at[:, others, :], back_send.at[0])
        drain(kept.at[:, others, :], back_send.at[1])

    @pl.when(jnp.logical_not(is_hub))
    def _():
        drain(grad, send_sem)


def totals_kernel(n, shares, totals, landed, mine, send_sem, recv_sem, back_send, back_recv):
    me = lax.axis_index("rows")
    meet(n, me)
    pltpu.make_async_copy(shares.at[me], landed.at[me], recv_sem).start()

    @pl.loop(1, n)
    def _(s):
        rank = lax.rem(me + s, n)
        send(shares.at[rank], landed.at[me], send_sem, recv_sem, rank)

    drain(landed, recv_sem)
    mine[...] = jnp.sum(landed[...].astype(jnp.float32), axis=0).astype(mine.dtype)
    pltpu.make_async_copy(mine, totals.at[me], back_recv).start()

    @pl.loop(1, n)
    def _(s):
        rank = lax.rem(me + s, n)
        send(mine, totals.at[me], back_send, back_recv, rank)

    drain(totals, back_recv)
    others = pl.ds(0, n - 1)
    drain(shares.at[others], send_sem)
    drain(shares.at[others], back_send)


def in_vmem(count):
    return [pl.BlockSpec(memory_space=pltpu.VMEM)] * count


def params(collective_id):
    return pltpu.CompilerParams(
        collective_id=collective_id, has_side_effects=True, vmem_limit_bytes=VMEM_LIMIT
    )


def exchange_forward(left, right, n):
    hubs, width, rows, residues = left.shape
    chunks = min(CHUNKS, width)
    return pl.pallas_call(
        functools.partial(forward_kernel, n),
        out_shape=[
            jax.ShapeDtypeStruct((hubs, width, rows, n * rows), jnp.bfloat16),
            jax.ShapeDtypeStruct((width, n // 2 * rows, residues), jnp.bfloat16),
            jax.ShapeDtypeStruct((width, n * rows, residues), jnp.bfloat16),
        ],
        in_specs=in_vmem(2),
        out_specs=in_vmem(3),
        scratch_shapes=[
            pltpu.VMEM((width, n // 2 * rows, n * rows), jnp.bfloat16),
            pltpu.SemaphoreType.DMA((2,)),
            pltpu.SemaphoreType.DMA((2, chunks)),
            pltpu.SemaphoreType.DMA,
            pltpu.SemaphoreType.DMA((chunks,)),
            pltpu.SemaphoreType.DMA,
            pltpu.SemaphoreType.DMA,
        ],
        compiler_params=params(0),
    )(left, right)


def exchange_backward(grad, left_held, right_held, n):
    hubs, width, rows, _ = grad.shape
    residues = left_held.shape[2]
    chunks = min(CHUNKS, width)
    slab = (width, n // 2 * rows, residues)
    back = jax.ShapeDtypeStruct((hubs, width, rows, residues), jnp.bfloat16)
    return pl.pallas_call(
        functools.partial(backward_kernel, n),
        out_shape=[back, back],
        in_specs=in_vmem(3),
        out_specs=in_vmem(2),
        scratch_shapes=[pltpu.VMEM((width, n // 2 * rows, n * rows), jnp.bfloat16)]
        + [pltpu.VMEM(slab, jnp.bfloat16)] * 4
        + [
            pltpu.SemaphoreType.DMA,
            pltpu.SemaphoreType.DMA((chunks,)),
            pltpu.SemaphoreType.DMA,
            pltpu.SemaphoreType.DMA((chunks,)),
            pltpu.SemaphoreType.DMA((2,)),
            pltpu.SemaphoreType.DMA((2,)),
        ],
        compiler_params=params(1),
    )(grad, left_held, right_held)


def sum_over_rows(shares, n):
    count, chans, _ = shares.shape
    rows = count * chans // n
    dtype = jnp.bfloat16 if rows % 16 == 0 else jnp.float32
    shares = shares.astype(jnp.bfloat16).astype(dtype).reshape(n, rows, chans)
    totals = pl.pallas_call(
        functools.partial(totals_kernel, n),
        out_shape=jax.ShapeDtypeStruct(shares.shape, dtype),
        in_specs=in_vmem(1),
        out_specs=pl.BlockSpec(memory_space=pltpu.VMEM),
        scratch_shapes=[
            pltpu.VMEM(shares.shape, dtype),
            pltpu.VMEM((rows, chans), dtype),
            pltpu.SemaphoreType.DMA,
            pltpu.SemaphoreType.DMA,
            pltpu.SemaphoreType.DMA,
            pltpu.SemaphoreType.DMA,
        ],
        compiler_params=params(2),
    )(shares)
    return totals.reshape(count, chans, chans).astype(jnp.float32)


def body(pair, proj_weights, cotangent):
    residues = pair.shape[1]
    local_rows = pair.shape[0]
    chans = pair.shape[2]
    ranks = lax.axis_size("rows")
    hubs = ranks // 4
    slab_width = chans // hubs
    normed_in, scale_in = layer_norm(pair.astype(jnp.float32), 2)
    normed_bf = normed_in.astype(jnp.bfloat16)
    edge_pre = jnp.einsum(
        "ikd,ndc->ncik", normed_bf, proj_weights[0:4], preferred_element_type=jnp.float32
    )
    gate_pre = jnp.einsum(
        "ikd,dc->ikc", normed_bf, proj_weights[4], preferred_element_type=jnp.float32
    )
    left_sig = jax.nn.sigmoid(edge_pre[1])
    right_sig = jax.nn.sigmoid(edge_pre[3])
    left_edge = (
        (left_sig * edge_pre[0])
        .astype(jnp.bfloat16)
        .reshape(hubs, slab_width, local_rows, residues)
    )
    right_edge = (
        (right_sig * edge_pre[2])
        .astype(jnp.bfloat16)
        .reshape(hubs, slab_width, local_rows, residues)
    )
    regrouped, left_held, right_held = exchange_forward(left_edge, right_edge, ranks)
    regrouped = regrouped.reshape(chans, local_rows, residues)
    normed_mid, scale_mid = layer_norm(regrouped.astype(jnp.float32), 0)
    mid_bf = normed_mid.astype(jnp.bfloat16)
    projected = jnp.einsum(
        "cij,cd->ijd", mid_bf, proj_weights[5], preferred_element_type=jnp.float32
    )
    gating = jax.nn.sigmoid(gate_pre)
    update = (gating * projected).astype(jnp.bfloat16)
    upstream = cotangent.astype(jnp.float32)
    gated_up = (upstream * gating).astype(jnp.bfloat16)
    gate_grad = (upstream * projected * gating * (1.0 - gating)).astype(jnp.bfloat16)
    out_weights = jnp.stack(
        [
            jnp.einsum("ikd,ikc->dc", normed_bf, gate_grad, preferred_element_type=jnp.float32),
            jnp.einsum("cij,ijd->cd", mid_bf, gated_up, preferred_element_type=jnp.float32),
        ]
    )
    mid_grad = jnp.einsum(
        "ijd,cd->cij", gated_up, proj_weights[5], preferred_element_type=jnp.float32
    )
    prod_grad = norm_backward(normed_mid, scale_mid, mid_grad, 0).astype(jnp.bfloat16)
    prod_grad = prod_grad.reshape(hubs, slab_width, local_rows, residues)
    left_back, right_back = exchange_backward(prod_grad, left_held, right_held, ranks)
    left_full = left_back.reshape(chans, local_rows, residues).astype(jnp.float32)
    right_full = right_back.reshape(chans, local_rows, residues).astype(jnp.float32)
    edge_grad = jnp.stack(
        [
            left_full * left_sig,
            left_full * edge_pre[0] * left_sig * (1.0 - left_sig),
            right_full * right_sig,
            right_full * edge_pre[2] * right_sig * (1.0 - right_sig),
        ]
    ).astype(jnp.bfloat16)
    in_weights = jnp.einsum(
        "ikd,ncik->ndc", normed_bf, edge_grad, preferred_element_type=jnp.float32
    )
    input_grad = jnp.einsum(
        "ncik,ndc->ikd", edge_grad, proj_weights[0:4], preferred_element_type=jnp.float32
    )
    input_grad = input_grad + jnp.einsum(
        "ikc,dc->ikd", gate_grad, proj_weights[4], preferred_element_type=jnp.float32
    )
    pair_grad = norm_backward(normed_in, scale_in, input_grad, 2).astype(jnp.bfloat16)
    totals = sum_over_rows(jnp.concatenate([in_weights, out_weights], axis=0), ranks)
    weight_grads = totals / residues
    return (update, pair_grad, weight_grads)


def solution(mesh):
    in_specs = (P(("groups", "rows"), None, None), P(), P(("groups", "rows"), None, None))
    out_specs = (
        P(("groups", "rows"), None, None),
        P(("groups", "rows"), None, None),
        P("groups", None, None),
    )
    return jax.shard_map(body, mesh=mesh, in_specs=in_specs, out_specs=out_specs, check_vma=False)
```

```python
import functools

import jax
import jax.numpy as jnp
from jax import lax
from jax.experimental import pallas as pl
from jax.experimental.pallas import tpu as pltpu
from jax.sharding import PartitionSpec as P

VMEM_LIMIT = 48 * 1024 * 1024
EDGE = (2, 2, 2, 2)
FORWARD_CHUNK = 2
BACKWARD_CHUNK = 4


def cut(width, inner):
    room = width - 2 * sum(EDGE)
    if room < 0 or room % inner:
        sizes = (1,) * width
    else:
        sizes = EDGE + (inner,) * (room // inner) + EDGE[::-1]
    bounds = [sum(sizes[:g]) for g in range(len(sizes) + 1)]
    return list(zip(bounds[:-1], bounds[1:]))


def layer_norm(values, along_dim):
    centred = values - jnp.mean(values, axis=along_dim, keepdims=True)
    inv_scale = lax.rsqrt(jnp.mean(centred * centred, axis=along_dim, keepdims=True) + 1e-05)
    return (centred * inv_scale, inv_scale)


def norm_backward(normed, inv_scale, upstream, along_dim):
    return (
        upstream
        - jnp.mean(upstream, axis=along_dim, keepdims=True)
        - normed * jnp.mean(upstream * normed, axis=along_dim, keepdims=True)
    ) * inv_scale


def meet(n, me):
    barrier = pltpu.get_barrier_semaphore()

    @pl.loop(1, n)
    def _(s):
        pl.semaphore_signal(
            barrier,
            inc=1,
            device_id={"rows": lax.rem(me + s, n)},
            device_id_type=pl.DeviceIdType.MESH,
        )

    pl.semaphore_wait(barrier, n - 1)


def send(src, dst, send_sem, recv_sem, rank):
    pltpu.make_async_remote_copy(
        src_ref=src,
        dst_ref=dst,
        send_sem=send_sem,
        recv_sem=recv_sem,
        device_id={"rows": rank},
        device_id_type=pl.DeviceIdType.MESH,
    ).start()


def drain(ref, sem):
    pltpu.make_async_copy(ref, ref, sem).wait()


def place(n):
    me = lax.axis_index("rows")
    half = lax.div(me, n // 2)
    first = half * (n // 2)
    hub = n // 4 * (1 + half)
    is_hub = jnp.logical_and(me >= hub, me < hub + n // 4)
    partner = me + n // 4 * (1 - 2 * half)
    return me, half, first, hub, is_hub, partner


def meet_partners(n, me, first, hub, is_hub, partner):
    barrier = pltpu.get_barrier_semaphore()

    def greet(rank):
        pl.semaphore_signal(
            barrier, inc=1, device_id={"rows": rank}, device_id_type=pl.DeviceIdType.MESH
        )

    @pl.when(is_hub)
    def _():
        @pl.loop(1, n // 2)
        def _(s):
            greet(first + lax.rem(me - first + s, n // 2))

        greet(partner)
        pl.semaphore_wait(barrier, n // 2)

    @pl.when(jnp.logical_not(is_hub))
    def _():
        @pl.loop(0, n // 4)
        def _(s):
            greet(hub + s)

        pl.semaphore_wait(barrier, n // 4)


def to_hubs(me, hub, hubs, is_hub, pairs, part, send_sems, recv_sems):
    @pl.loop(0, hubs)
    def _(s):
        q = lax.rem(me + s, hubs)

        @pl.when(hub + q != me)
        def _():
            for (src, dst), sent, came in zip(pairs, send_sems, recv_sems):
                send(src.at[q, part], dst, sent, came, hub + q)

    @pl.when(is_hub)
    def _():
        for (src, dst), came in zip(pairs, recv_sems):
            pltpu.make_async_copy(src.at[me - hub, part], dst, came).start()


def from_hub(me, first, hub, members, rows, pairs, part, send_sems, recv_sems):
    for (src, dst), came in zip(pairs, recv_sems):
        pltpu.make_async_copy(
            src.at[part, pl.ds((me - first) * rows, rows), :], dst.at[me - hub, part], came
        ).start()

    @pl.loop(1, members)
    def _(s):
        member = lax.rem(me - first + s, members)
        for (src, dst), sent, came in zip(pairs, send_sems, recv_sems):
            send(
                src.at[part, pl.ds(member * rows, rows), :],
                dst.at[me - hub, part],
                sent,
                came,
                first + member,
            )


def forward_kernel(
    n, left, right, regrouped, left_held, right_held, products,
    send_sem, recv_sem, swap_send, swap_recv, back_send, back_recv
):
    me, half, first, hub, is_hub, partner = place(n)
    hubs, width, rows, _ = left.shape
    members = n // 2
    bounds = cut(width, FORWARD_CHUNK)
    chunks = len(bounds)
    parts = [pl.ds(a, b - a) for a, b in bounds]
    meet_partners(n, me, first, hub, is_hub, partner)
    own_rows = pl.ds(first * rows, members * rows)
    far_rows = pl.ds((members - first) * rows, members * rows)
    for g in range(chunks):
        part = parts[g]
        pairs = (
            (right, right_held.at[part, pl.ds(me * rows, rows), :]),
            (left, left_held.at[part, pl.ds((me - first) * rows, rows), :]),
        )
        to_hubs(
            me, hub, hubs, is_hub, pairs, part,
            (send_sem.at[1], send_sem.at[0]), (recv_sem.at[1, g], recv_sem.at[0, g]),
        )

    @pl.when(is_hub)
    def _():
        for g in range(chunks + 1):
            if g < chunks:
                part = parts[g]
                block = right_held.at[part, own_rows, :]
                drain(block, recv_sem.at[1, g])
                send(block, block, swap_send, swap_recv.at[g], partner)
            if g > 0:
                done = parts[g - 1]
                drain(left_held.at[done], recv_sem.at[0, g - 1])
                drain(right_held.at[done, far_rows, :], swap_recv.at[g - 1])

                @pl.loop(*bounds[g - 1])
                def _(c):
                    products[c] = lax.dot_general(
                        left_held[c], right_held[c], (((1,), (1,)), ((), ())),
                        preferred_element_type=jnp.float32,
                    ).astype(jnp.bfloat16)

                from_hub(
                    me, first, hub, members, rows, ((products, regrouped),), done,
                    (back_send,), (back_recv,),
                )

    drain(regrouped, back_recv)

    @pl.when(is_hub)
    def _():
        others = pl.ds(0, hubs - 1)
        drain(left.at[others], send_sem.at[0])
        drain(right.at[others], send_sem.at[1])
        drain(left_held, swap_send)
        drain(products.at[:, pl.ds(0, (members - 1) * rows), :], back_send)

    @pl.when(jnp.logical_not(is_hub))
    def _():
        drain(left, send_sem.at[0])
        drain(right, send_sem.at[1])


def backward_kernel(
    n, grad, left_held, right_held, left_back, right_back,
    held, left_part, kept, away, landed,
    send_sem, recv_sem, swap_send, swap_recv, back_send, back_recv
):
    me, half, first, hub, is_hub, partner = place(n)
    hubs, width, rows, _ = grad.shape
    members = n // 2
    bounds = cut(width, BACKWARD_CHUNK)
    chunks = len(bounds)
    parts = [pl.ds(a, b - a) for a, b in bounds]
    meet_partners(n, me, first, hub, is_hub, partner)
    span = members * rows
    own_cols = pl.ds(pl.multiple_of(first * rows, span), span)
    far_cols = pl.ds(pl.multiple_of((members - first) * rows, span), span)
    for g in range(chunks):
        part = parts[g]
        pairs = ((grad, held.at[part, pl.ds((me - first) * rows, rows), :]),)
        to_hubs(me, hub, hubs, is_hub, pairs, part, (send_sem,), (recv_sem.at[g],))

    def outer(upstream, values):
        return lax.dot_general(
            upstream, values, (((0,), (0,)), ((), ())), preferred_element_type=jnp.float32
        ).astype(jnp.bfloat16)

    @pl.when(is_hub)
    def _():
        for g in range(chunks + 1):
            if g < chunks:
                part = parts[g]
                drain(held.at[part], recv_sem.at[g])

                @pl.loop(*bounds[g])
                def _(c):
                    away[c] = outer(held[c, :, far_cols], left_held[c])

                send(away.at[part], landed.at[part], swap_send, swap_recv.at[g], partner)

                @pl.loop(*bounds[g])
                def _(c):
                    left_part[c] = lax.dot_general(
                        held[c], right_held[c], (((1,), (0,)), ((), ())),
                        preferred_element_type=jnp.float32,
                    ).astype(jnp.bfloat16)
                    kept[c] = outer(held[c, :, own_cols], left_held[c])

                from_hub(
                    me, first, hub, members, rows, ((left_part, left_back),), part,
                    (back_send.at[0],), (back_recv.at[0],),
                )
            if g > 0:
                done = parts[g - 1]
                drain(landed.at[done], swap_recv.at[g - 1])

                @pl.loop(*bounds[g - 1])
                def _(c):
                    kept[c] = (
                        kept[c].astype(jnp.float32) + landed[c].astype(jnp.float32)
                    ).astype(jnp.bfloat16)

                from_hub(
                    me, first, hub, members, rows, ((kept, right_back),), done,
                    (back_send.at[1],), (back_recv.at[1],),
                )

    drain(left_back, back_recv.at[0])
    drain(right_back, back_recv.at[1])

    @pl.when(is_hub)
    def _():
        drain(grad.at[pl.ds(0, hubs - 1)], send_sem)
        drain(away, swap_send)
        others = pl.ds(0, (members - 1) * rows)
        drain(left_part.at[:, others, :], back_send.at[0])
        drain(kept.at[:, others, :], back_send.at[1])

    @pl.when(jnp.logical_not(is_hub))
    def _():
        drain(grad, send_sem)


def totals_kernel(n, shares, totals, landed, mine, send_sem, recv_sem, back_send, back_recv):
    me = lax.axis_index("rows")
    meet(n, me)
    pltpu.make_async_copy(shares.at[me], landed.at[me], recv_sem).start()

    @pl.loop(1, n)
    def _(s):
        rank = lax.rem(me + s, n)
        send(shares.at[rank], landed.at[me], send_sem, recv_sem, rank)

    drain(landed, recv_sem)
    mine[...] = jnp.sum(landed[...].astype(jnp.float32), axis=0).astype(mine.dtype)
    pltpu.make_async_copy(mine, totals.at[me], back_recv).start()

    @pl.loop(1, n)
    def _(s):
        rank = lax.rem(me + s, n)
        send(mine, totals.at[me], back_send, back_recv, rank)

    drain(totals, back_recv)
    others = pl.ds(0, n - 1)
    drain(shares.at[others], send_sem)
    drain(shares.at[others], back_send)


def in_vmem(count):
    return [pl.BlockSpec(memory_space=pltpu.VMEM)] * count


def params(collective_id):
    return pltpu.CompilerParams(
        collective_id=collective_id, has_side_effects=True, vmem_limit_bytes=VMEM_LIMIT
    )


def exchange_forward(left, right, n):
    hubs, width, rows, residues = left.shape
    chunks = len(cut(width, FORWARD_CHUNK))
    return pl.pallas_call(
        functools.partial(forward_kernel, n),
        out_shape=[
            jax.ShapeDtypeStruct((hubs, width, rows, n * rows), jnp.bfloat16),
            jax.ShapeDtypeStruct((width, n // 2 * rows, residues), jnp.bfloat16),
            jax.ShapeDtypeStruct((width, n * rows, residues), jnp.bfloat16),
        ],
        in_specs=in_vmem(2),
        out_specs=in_vmem(3),
        scratch_shapes=[
            pltpu.VMEM((width, n // 2 * rows, n * rows), jnp.bfloat16),
            pltpu.SemaphoreType.DMA((2,)),
            pltpu.SemaphoreType.DMA((2, chunks)),
            pltpu.SemaphoreType.DMA,
            pltpu.SemaphoreType.DMA((chunks,)),
            pltpu.SemaphoreType.DMA,
            pltpu.SemaphoreType.DMA,
        ],
        compiler_params=params(0),
    )(left, right)


def exchange_backward(grad, left_held, right_held, n):
    hubs, width, rows, _ = grad.shape
    residues = left_held.shape[2]
    chunks = len(cut(width, BACKWARD_CHUNK))
    slab = (width, n // 2 * rows, residues)
    back = jax.ShapeDtypeStruct((hubs, width, rows, residues), jnp.bfloat16)
    return pl.pallas_call(
        functools.partial(backward_kernel, n),
        out_shape=[back, back],
        in_specs=in_vmem(3),
        out_specs=in_vmem(2),
        scratch_shapes=[pltpu.VMEM((width, n // 2 * rows, n * rows), jnp.bfloat16)]
        + [pltpu.VMEM(slab, jnp.bfloat16)] * 4
        + [
            pltpu.SemaphoreType.DMA,
            pltpu.SemaphoreType.DMA((chunks,)),
            pltpu.SemaphoreType.DMA,
            pltpu.SemaphoreType.DMA((chunks,)),
            pltpu.SemaphoreType.DMA((2,)),
            pltpu.SemaphoreType.DMA((2,)),
        ],
        compiler_params=params(1),
    )(grad, left_held, right_held)


def sum_over_rows(shares, n):
    count, chans, _ = shares.shape
    rows = count * chans // n
    dtype = jnp.bfloat16 if rows % 16 == 0 else jnp.float32
    shares = shares.astype(jnp.bfloat16).astype(dtype).reshape(n, rows, chans)
    totals = pl.pallas_call(
        functools.partial(totals_kernel, n),
        out_shape=jax.ShapeDtypeStruct(shares.shape, dtype),
        in_specs=in_vmem(1),
        out_specs=pl.BlockSpec(memory_space=pltpu.VMEM),
        scratch_shapes=[
            pltpu.VMEM(shares.shape, dtype),
            pltpu.VMEM((rows, chans), dtype),
            pltpu.SemaphoreType.DMA,
            pltpu.SemaphoreType.DMA,
            pltpu.SemaphoreType.DMA,
            pltpu.SemaphoreType.DMA,
        ],
        compiler_params=params(2),
    )(shares)
    return totals.reshape(count, chans, chans).astype(jnp.float32)


def body(pair, proj_weights, cotangent):
    residues = pair.shape[1]
    local_rows = pair.shape[0]
    chans = pair.shape[2]
    ranks = lax.axis_size("rows")
    hubs = ranks // 4
    slab_width = chans // hubs
    normed_in, scale_in = layer_norm(pair.astype(jnp.float32), 2)
    normed_bf = normed_in.astype(jnp.bfloat16)
    edge_pre = jnp.einsum(
        "ikd,ndc->ncik", normed_bf, proj_weights[0:4], preferred_element_type=jnp.float32
    )
    gate_pre = jnp.einsum(
        "ikd,dc->ikc", normed_bf, proj_weights[4], preferred_element_type=jnp.float32
    )
    left_sig = jax.nn.sigmoid(edge_pre[1])
    right_sig = jax.nn.sigmoid(edge_pre[3])
    left_edge = (
        (left_sig * edge_pre[0])
        .astype(jnp.bfloat16)
        .reshape(hubs, slab_width, local_rows, residues)
    )
    right_edge = (
        (right_sig * edge_pre[2])
        .astype(jnp.bfloat16)
        .reshape(hubs, slab_width, local_rows, residues)
    )
    regrouped, left_held, right_held = exchange_forward(left_edge, right_edge, ranks)
    regrouped = regrouped.reshape(chans, local_rows, residues)
    normed_mid, scale_mid = layer_norm(regrouped.astype(jnp.float32), 0)
    mid_bf = normed_mid.astype(jnp.bfloat16)
    projected = jnp.einsum(
        "cij,cd->ijd", mid_bf, proj_weights[5], preferred_element_type=jnp.float32
    )
    gating = jax.nn.sigmoid(gate_pre)
    update = (gating * projected).astype(jnp.bfloat16)
    upstream = cotangent.astype(jnp.float32)
    gated_up = (upstream * gating).astype(jnp.bfloat16)
    gate_grad = (upstream * projected * gating * (1.0 - gating)).astype(jnp.bfloat16)
    out_weights = jnp.stack(
        [
            jnp.einsum("ikd,ikc->dc", normed_bf, gate_grad, preferred_element_type=jnp.float32),
            jnp.einsum("cij,ijd->cd", mid_bf, gated_up, preferred_element_type=jnp.float32),
        ]
    )
    mid_grad = jnp.einsum(
        "ijd,cd->cij", gated_up, proj_weights[5], preferred_element_type=jnp.float32
    )
    prod_grad = norm_backward(normed_mid, scale_mid, mid_grad, 0).astype(jnp.bfloat16)
    prod_grad = prod_grad.reshape(hubs, slab_width, local_rows, residues)
    left_back, right_back = exchange_backward(prod_grad, left_held, right_held, ranks)
    left_full = left_back.reshape(chans, local_rows, residues).astype(jnp.float32)
    right_full = right_back.reshape(chans, local_rows, residues).astype(jnp.float32)
    edge_grad = jnp.stack(
        [
            left_full * left_sig,
            left_full * edge_pre[0] * left_sig * (1.0 - left_sig),
            right_full * right_sig,
            right_full * edge_pre[2] * right_sig * (1.0 - right_sig),
        ]
    ).astype(jnp.bfloat16)
    in_weights = jnp.einsum(
        "ikd,ncik->ndc", normed_bf, edge_grad, preferred_element_type=jnp.float32
    )
    input_grad = jnp.einsum(
        "ncik,ndc->ikd", edge_grad, proj_weights[0:4], preferred_element_type=jnp.float32
    )
    input_grad = input_grad + jnp.einsum(
        "ikc,dc->ikd", gate_grad, proj_weights[4], preferred_element_type=jnp.float32
    )
    pair_grad = norm_backward(normed_in, scale_in, input_grad, 2).astype(jnp.bfloat16)
    totals = sum_over_rows(jnp.concatenate([in_weights, out_weights], axis=0), ranks)
    weight_grads = totals / residues
    return (update, pair_grad, weight_grads)


def solution(mesh):
    in_specs = (P(("groups", "rows"), None, None), P(), P(("groups", "rows"), None, None))
    out_specs = (
        P(("groups", "rows"), None, None),
        P(("groups", "rows"), None, None),
        P("groups", None, None),
    )
    return jax.shard_map(body, mesh=mesh, in_specs=in_specs, out_specs=out_specs, check_vma=False)
```
